256 devices in a mesh: grp: 8 (over x, core), dev: 32 (over y, z).
Axes of the slice: x: 4, y: 4, z: 8, core: 2. Of those that a mesh axis runs over, the one named last changes fastest.
Arguments:
- queries: bfloat16 [1024, 16, 4096], P(('grp', 'dev')), may hold values from -25.849872 to 25.849872
- own_keys: bfloat16 [1024, 16, 1024], P(('grp', 'dev')), may hold values from -18 to 18
- own_values: bfloat16 [1024, 16, 1024], P(('grp', 'dev')), may hold values from -48 to 48
- prefix_keys: bfloat16 [1024, 1024], P('grp'), may hold values from -6 to 6
- prefix_values: bfloat16 [1024, 1024], P('grp'), may hold values from -48 to 48
- passage_keys: bfloat16 [32, 512, 1024], P('dev'), may hold values from -6 to 6
- passage_values: bfloat16 [32, 512, 1024], P('dev'), may hold values from -48 to 48
- retrieval: int32 [1024, 8], P(('grp', 'dev')), may hold values from 0 to 31, all different within a row; in each aligned block of 4 rows (0 to 3, 4 to 7, ...) at most 2 rows name the same one
- location: int32 [32], replicated, may hold values from 0 to 31, each once
Outputs:
- attended: bfloat16 [1024, 16, 4096], P(('grp', 'dev'))
The draws below stay inside these ranges and needn't reach their ends.
Inputs may be any that keep to these rules, and one draw needn't show every extreme that they name: `retrieval`: each response names 8 different passages. The 4 responses of one device name one passage at most 2 times together, and on some devices some passage exactly 2 times. `location`: each position is taken by exactly one passage.
All inputs are finite; a program needn't handle non-finite values.
Results may differ from the reference program's by a relative error of at most 0.004.
Values may be sent and summed in bfloat16 or wider, within the bound.
No kernel may reach another device: no remote copies, remote signals or barrier semaphores. Data moves between devices by JAX's collectives and lax.ppermute only.
A program may use at most 192 MiB of HBM per device.

```python
import math
import jax
import jax.numpy as jnp
import numpy as np
from jax import lax

HEADS = 32
KEY_VALUE_HEADS = 8
HEAD_WIDTH = 128
PASS_TOK = 512
PREFIX = 1024
TOPK = 8
RESP_TOK = 16
RESP_DEV = 4
PASSAGES = 32
RESPONSES = 1024
MOST = 2


def draw_queries(key, part):
    key = jax.random.fold_in(key, 101)
    shape = (RESPONSES, RESP_TOK, HEADS * HEAD_WIDTH)
    values = jnp.clip(jax.random.normal(key, shape, jnp.float32), -6.0, 6.0)
    return values.astype(jnp.bfloat16)


def draw_own_keys(key, part):
    key = jax.random.fold_in(key, 202)
    shape = (RESPONSES, RESP_TOK, KEY_VALUE_HEADS * HEAD_WIDTH)
    values = jnp.clip(3.0 * jax.random.normal(key, shape, jnp.float32), -18.0, 18.0)
    return values.astype(jnp.bfloat16)


def steps_of(own_key, extent, shards, smallest, high):
    loudness = 1.0
    for dim, shards_of in shards:
        heights = jax.random.uniform(jax.random.fold_in(jax.random.fold_in(own_key, 6), dim), (shards_of,), jnp.float32, smallest / len(shards), high / len(shards))
        loudness = loudness * jnp.repeat(jnp.exp(heights), extent[dim] // shards_of).reshape((-1,) + (1,) * (len(extent) - 1 - dim))
    return loudness


def assign_block(key, own, number, rows, count, top, most, slope):
    sequence = jax.random.permutation(key, count)
    packed, common = portions_of(count, rows * top, most, slope, True), portions_of(count, rows * top, most, slope, False)
    places = jnp.arange(count)

    def named(sizes, rotation):
        used = int((sizes > 0).sum())
        fixed = max(1, used // 4)
        shifted = fixed + (places - fixed + rotation * (used - fixed)) % max(1, count - fixed)
        return jnp.zeros((count,), jnp.int32).at[sequence[jnp.where(places < fixed, places, shifted)]].set(jnp.asarray(sizes, jnp.int32))

    sizes = jnp.where(number % 4 == 0, named(packed, number // 4), named(common, number - number // 4 - 1))
    mixed = jax.random.permutation(jax.random.fold_in(own, 3), count)
    giver, sink = mixed[0:count // 2 * 2:2], mixed[1:count // 2 * 2:2]
    margin = jnp.minimum(sizes[giver] - 1, most - sizes[sink]) // 2
    margin = jnp.where((giver == sequence[0]) | (sink == sequence[0]) | (sizes[sink] == 0), 0, jnp.maximum(margin, 0))
    shifted = jax.random.randint(jax.random.fold_in(own, 4), (count // 2,), 0, 1 << 20) % (margin + 1)
    sizes = sizes.at[giver].add(-shifted).at[sink].add(shifted)
    items = jnp.searchsorted(jnp.cumsum(sizes), jnp.arange(rows * top), side="right").astype(jnp.int32)
    table = items.reshape(top, rows).T
    table = table[jax.random.permutation(jax.random.fold_in(own, 1), rows)]
    rotation = jax.random.randint(jax.random.fold_in(own, 2), (rows, 1), 0, top)
    return jnp.take_along_axis(table, (jnp.arange(top)[None, :] + rotation) % top, axis=1)


def portions_of(amount, total, limit, skew, full):
    loads = [(1 << 20) // math.isqrt(grade ** skew) + 1 for grade in range(1, amount + 1)]
    largest = limit if full else min(limit, max(-(-total // amount), total * loads[0] // sum(loads)))
    least = 1 if total - largest >= amount - 1 else 0
    holding, spare = [largest] + [least] * (amount - 1), total - largest - least * (amount - 1)
    while spare > 0:
        free = [i for i in range(1, amount) if holding[i] < largest] or [i for i in range(1, amount) if holding[i] < limit]
        whole, remaining = sum([loads[i] for i in free]), spare
        for i in free:
            more = min(limit - holding[i], max(1, remaining * loads[i] // whole), spare)
            holding[i] = holding[i] + more
            spare = spare - more
    return np.array(holding)


def scatter_about(key, extent, spread, most, cuts=(), dtype=jnp.bfloat16):
    loudness = steps_of(key, extent, cuts, -0.22, 0.18) if cuts else 1.0
    entries = jax.random.normal(key, extent, jnp.float32) * spread * loudness
    return jnp.minimum(jnp.maximum(entries, -most), most).astype(dtype)


def setup_inputs(seed: int = 0) -> dict:
    keys = jax.random.split(jax.random.key(seed), 10)
    queries = draw_queries(jax.random.fold_in(keys[9], 71), 0)
    own_keys = draw_own_keys(jax.random.fold_in(keys[9], 71), 0)
    own_values = scatter_about(keys[2], (RESPONSES, RESP_TOK, KEY_VALUE_HEADS * HEAD_WIDTH), 8.0, 48.0, ((0, 256),))
    prefix_keys = scatter_about(keys[3], (PREFIX, KEY_VALUE_HEADS * HEAD_WIDTH), 1.0, 6.0, ((0, 8),))
    prefix_values = scatter_about(keys[4], (PREFIX, KEY_VALUE_HEADS * HEAD_WIDTH), 8.0, 48.0, ((0, 8),))
    passage_keys = scatter_about(keys[5], (PASSAGES, PASS_TOK, KEY_VALUE_HEADS * HEAD_WIDTH), 1.0, 6.0, ((0, 32),))
    passage_values = scatter_about(keys[6], (PASSAGES, PASS_TOK, KEY_VALUE_HEADS * HEAD_WIDTH), 8.0, 48.0, ((0, 32),))
    retrieval_keys = jax.random.split(jax.random.fold_in(keys[7], 1), RESPONSES // RESP_DEV)
    retrieval_turns = jax.random.permutation(jax.random.fold_in(keys[7], 3), RESPONSES // RESP_DEV)
    retrieval = jax.vmap(lambda own, number: assign_block(jax.random.fold_in(keys[7], 2), own, number, RESP_DEV, PASSAGES, TOPK, MOST, 2))(retrieval_keys, retrieval_turns).reshape((RESPONSES, TOPK))
    location = jax.random.permutation(keys[8], PASSAGES).astype(jnp.int32)
    return {"queries": queries, "own_keys": own_keys, "own_values": own_values, "prefix_keys": prefix_keys, "prefix_values": prefix_values, "passage_keys": passage_keys, "passage_values": passage_values, "retrieval": retrieval, "location": location}


def softmax_part(scores, values, form):
    maxima = jnp.max(scores, axis=-1)
    weights = jnp.exp(scores - maxima[..., None])
    totals = jnp.sum(weights, axis=-1)
    rounded = lax.optimization_barrier(weights.astype(jnp.bfloat16)).astype(jnp.float32)
    mixed = jnp.einsum(form, rounded, values.astype(jnp.float32))
    return mixed / totals[..., None], maxima + jnp.log(totals)


def reference(queries, own_keys, own_values, prefix_keys, prefix_values, passage_keys, passage_values, retrieval, location):
    query_group = HEADS // KEY_VALUE_HEADS
    scale = 1.0 / (HEAD_WIDTH ** 0.5)
    pre_keys = prefix_keys.astype(jnp.float32).reshape(PREFIX, KEY_VALUE_HEADS, HEAD_WIDTH)
    pre_values = prefix_values.reshape(PREFIX, KEY_VALUE_HEADS, HEAD_WIDTH)
    causal = jnp.arange(RESP_TOK)[:, None] >= jnp.arange(RESP_TOK)[None, :]

    def one_response(items):
        query, keys_own, values_own, chosen_ids = items
        grid = query.astype(jnp.float32).reshape(RESP_TOK, KEY_VALUE_HEADS, query_group, HEAD_WIDTH)
        pre_scores = jnp.einsum("tkgd,skd->tkgs", grid, pre_keys) * scale
        pre_out, pre_lse = softmax_part(pre_scores, pre_values, "tkgs,skd->tkgd")
        own_grid = keys_own.astype(jnp.float32).reshape(RESP_TOK, KEY_VALUE_HEADS, HEAD_WIDTH)
        own_scores = jnp.einsum("tkgd,skd->tkgs", grid, own_grid) * scale
        own_scores = jnp.where(causal[:, None, None, :], own_scores, -jnp.inf)
        own_out, own_lse = softmax_part(own_scores, values_own.reshape(RESP_TOK, KEY_VALUE_HEADS, HEAD_WIDTH), "tkgs,skd->tkgd")
        positions = location[chosen_ids].astype(jnp.int32)
        chosen_keys = passage_keys[positions].astype(jnp.float32).reshape(TOPK, PASS_TOK, KEY_VALUE_HEADS, HEAD_WIDTH)
        chosen_values = passage_values[positions].reshape(TOPK, PASS_TOK, KEY_VALUE_HEADS, HEAD_WIDTH)
        pass_scores = jnp.einsum("tkgd,jskd->jtkgs", grid, chosen_keys) * scale
        pass_out, pass_lse = softmax_part(pass_scores, chosen_values, "jtkgs,jskd->jtkgd")
        pass_out = lax.optimization_barrier(pass_out.astype(jnp.bfloat16)).astype(jnp.float32)
        top = jnp.maximum(jnp.maximum(pre_lse, own_lse), jnp.max(pass_lse, axis=0))
        total = jnp.exp(pre_lse - top) + jnp.exp(own_lse - top) + jnp.sum(jnp.exp(pass_lse - top[None]), axis=0)
        level = top + jnp.log(total)
        result = jnp.exp(pre_lse - level)[..., None] * pre_out + jnp.exp(own_lse - level)[..., None] * own_out
        result = result + jnp.sum(jnp.exp(pass_lse - level[None])[..., None] * pass_out, axis=0)
        return result.reshape(RESP_TOK, HEADS * HEAD_WIDTH).astype(jnp.bfloat16)

    return lax.map(one_response, (queries, own_keys, own_values, retrieval), batch_size=16)
```

```python
import functools
import math

import jax
import jax.numpy as jnp
from jax import lax
from jax.experimental import pallas as pl
from jax.experimental.pallas import tpu as pltpu
from jax.sharding import PartitionSpec as P

HEADS = 32
KV = 8
D = 128
TOPK = 8
NX, NC, NY, NZ = 4, 2, 4, 8
AXES = ("grp", "dev")
RESP = 4
T = 16
GROUP = HEADS // KV
ROWS = GROUP * T
NR = 8 * RESP
SLOTS = NR + 1
BATCH = 4
COEF = math.log2(math.e) / math.sqrt(D)


def index_of(x, c, y, z):
    return ((x % NX) * NC + c) * (NY * NZ) + (y % NY) * NZ + z % NZ


def moves(to):
    places = [
        (x, c, y, z) for x in range(NX) for c in range(NC) for y in range(NY) for z in range(NZ)
    ]
    return [(index_of(*p), index_of(*to(*p))) for p in places]


def send(block, to):
    return lax.ppermute(block, AXES, moves(to))


def y_by(step):
    return lambda x, c, y, z: (x, c, y + step, z)


def z_by(step):
    return lambda x, c, y, z: (x, c, y, z + step)


def other_core(x, c, y, z):
    return (x, 1 - c, y, z)


def head_groups():
    return [
        [index_of(x, c, 2 * high + low, z) for x in range(NX) for low in range(2)]
        for c in range(NC)
        for high in range(2)
        for z in range(NZ)
    ]


def nt(a, b):
    return lax.dot_general(a, b, (((1,), (1,)), ((), ())), preferred_element_type=jnp.float32)


def first_kernel(got_ref, theirs_ref, q_ref, acc_ref, m_ref, keys, values):
    for s in range(8):
        at = pl.ds(s * 64, 64)
        keys[at, :] = got_ref[s, :, 768:896]
        values[at, 0:D] = got_ref[s, :, 896:1024]
        at = pl.ds(512 + s * 64, 64)
        keys[at, :] = theirs_ref[s, :, 0:D]
        values[at, 0:D] = theirs_ref[s, :, D : 2 * D]
    values[:, D:] = jnp.ones((1024, D), jnp.bfloat16)
    q_ref[NR * ROWS :, :] = jnp.zeros((ROWS, D), jnp.bfloat16)
    m_ref[NR * ROWS :, :] = jnp.zeros((ROWS, D), jnp.float32)
    acc_ref[NR * ROWS :, :] = jnp.zeros((ROWS, 2 * D), jnp.float32)
    row = lax.broadcasted_iota(jnp.int32, (RESP * ROWS, RESP * T), 0)
    col = lax.broadcasted_iota(jnp.int32, (RESP * ROWS, RESP * T), 1)
    seen = (row // ROWS == col // T) & (row % T >= col % T)

    @pl.loop(0, 8)
    def _(s):
        base = pl.multiple_of(s * (RESP * ROWS), RESP * ROWS)
        q = jnp.concatenate(
            [
                got_ref[s, a * T : (a + 1) * T, g * D : (g + 1) * D]
                for a in range(RESP)
                for g in range(GROUP)
            ],
            axis=0,
        )
        q_ref[pl.ds(base, RESP * ROWS), :] = q
        own = jnp.where(seen, nt(q, got_ref[s, :, 512:640]), -jnp.inf)
        far = nt(q, keys[...])
        top = jnp.maximum(
            jnp.max(far, axis=1, keepdims=True), jnp.max(own, axis=1, keepdims=True)
        )
        m = jnp.broadcast_to(top * COEF, (RESP * ROWS, D))
        p = jnp.concatenate(
            [
                jnp.exp2(far[:, j * D : (j + 1) * D] * COEF - m).astype(jnp.bfloat16)
                for j in range(8)
            ],
            axis=1,
        )
        po = jnp.exp2(own * COEF - m[:, : RESP * T]).astype(jnp.bfloat16)
        vo = jnp.concatenate(
            [got_ref[s, :, 640:768], jnp.ones((RESP * T, D), jnp.bfloat16)], axis=1
        )
        acc = jnp.dot(p, values[...], preferred_element_type=jnp.float32)
        acc = acc + jnp.dot(po, vo, preferred_element_type=jnp.float32)
        m_ref[pl.ds(base, RESP * ROWS), :] = m
        acc_ref[pl.ds(base, RESP * ROWS), :] = acc


def first_call(got, theirs):
    n = SLOTS * ROWS
    return pl.pallas_call(
        first_kernel,
        out_shape=(
            jax.ShapeDtypeStruct((n, D), jnp.bfloat16),
            jax.ShapeDtypeStruct((n, 2 * D), jnp.float32),
            jax.ShapeDtypeStruct((n, D), jnp.float32),
        ),
        in_specs=[pl.BlockSpec(memory_space=pltpu.VMEM)] * 2,
        out_specs=(pl.BlockSpec(memory_space=pltpu.VMEM),) * 3,
        scratch_shapes=[
            pltpu.VMEM((1024, D), jnp.bfloat16),
            pltpu.VMEM((1024, 2 * D), jnp.bfloat16),
        ],
        compiler_params=pltpu.CompilerParams(vmem_limit_bytes=24 * 1024 * 1024),
        cost_estimate=pl.CostEstimate(
            flops=4 * 2048 * 1088 * D, bytes_accessed=6 * 1024 * 1024, transcendentals=2048 * 1088
        ),
        name="prefix_and_own",
    )(got, theirs)


def passage_kernel(counts, last, places_ref, count_ref, list_ref, q_ref, acc_in, m_in, *rest):
    blocks = rest[: 2 * len(counts)]
    if last:
        out_ref, acc, m, values = rest[2 * len(counts) :]
    else:
        acc, m, values = rest[2 * len(counts) :]
    acc[...] = acc_in[...]
    m[...] = m_in[...]
    values[:, D:] = jnp.ones((512, D), jnp.bfloat16)
    first = 0
    for number, count in enumerate(counts):
        mine, theirs = blocks[2 * number], blocks[2 * number + 1]

        @pl.loop(0, count)
        def _(i, mine=mine, theirs=theirs, first=first):
            place = places_ref[first + i]
            values[0:256, 0:D] = mine[i, :, D:]
            values[256:512, 0:D] = theirs[i, :, D:]

            @pl.loop(0, (count_ref[place] + BATCH - 1) // BATCH)
            def _(b):
                at = [
                    pl.ds(pl.multiple_of(list_ref[place, b * BATCH + k] * ROWS, ROWS), ROWS)
                    for k in range(BATCH)
                ]
                q = jnp.concatenate([q_ref[a, :] for a in at], axis=0)
                sc = [nt(q, mine[i, :, 0:D]), nt(q, theirs[i, :, 0:D])]
                top = jnp.maximum(
                    jnp.max(sc[0], axis=1, keepdims=True), jnp.max(sc[1], axis=1, keepdims=True)
                )
                old = jnp.concatenate([m[a, :] for a in at], axis=0)
                new = jnp.maximum(old, top * COEF)
                shrink = jnp.exp2(old - new)
                p = jnp.concatenate(
                    [
                        jnp.exp2(h[:, j * D : (j + 1) * D] * COEF - new).astype(jnp.bfloat16)
                        for h in sc
                        for j in range(2)
                    ],
                    axis=1,
                )
                mixed = jnp.dot(p, values[...], preferred_element_type=jnp.float32)
                for k, a in enumerate(at):
                    part = slice(k * ROWS, (k + 1) * ROWS)
                    m[a, :] = new[part]
                    acc[a, 0:D] = acc[a, 0:D] * shrink[part] + mixed[part, 0:D]
                    acc[a, D:] = acc[a, D:] * shrink[part] + mixed[part, D:]

        first += count
    if last:

        @pl.loop(0, NR)
        def _(r):
            at = pl.ds(pl.multiple_of(r * ROWS, ROWS), ROWS)
            o = (acc[at, 0:D] / acc[at, D:]).astype(jnp.bfloat16)
            for g in range(GROUP):
                out_ref[pl.ds(pl.multiple_of(r * T, T), T), g * D : (g + 1) * D] = o[
                    g * T : (g + 1) * T
                ]


def passage_call(places, counts_of, lists, q, acc, m, pairs, last):
    n = SLOTS * ROWS
    counts = tuple(mine.shape[0] for mine, _ in pairs)
    total = sum(counts)
    state = (jax.ShapeDtypeStruct((n, 2 * D), jnp.float32), jax.ShapeDtypeStruct((n, D), jnp.float32))
    scratch = [pltpu.VMEM((512, 2 * D), jnp.bfloat16)]
    if last:
        out_shape = (jax.ShapeDtypeStruct((NR * T, GROUP * D), jnp.bfloat16),)
        scratch = [pltpu.VMEM((n, 2 * D), jnp.float32), pltpu.VMEM((n, D), jnp.float32)] + scratch
        aliases = {}
    else:
        out_shape = state
        aliases = {4: 0, 5: 1}
    vmem = pl.BlockSpec(memory_space=pltpu.VMEM)
    smem = pl.BlockSpec(memory_space=pltpu.SMEM)
    return pl.pallas_call(
        functools.partial(passage_kernel, counts, last),
        out_shape=out_shape,
        in_specs=[smem] * 3 + [vmem] * (3 + 2 * len(counts)),
        out_specs=(vmem,) * len(out_shape),
        scratch_shapes=scratch,
        input_output_aliases=aliases,
        compiler_params=pltpu.CompilerParams(vmem_limit_bytes=28 * 1024 * 1024),
        cost_estimate=pl.CostEstimate(
            flops=4 * total * 10 * ROWS * 512 * D,
            bytes_accessed=6 * 1024 * 1024,
            transcendentals=total * 10 * ROWS * 512,
        ),
        name="passages",
    )(places, counts_of, lists, q, acc, m, *[a for pair in pairs for a in pair])


def per_device(
    queries,
    own_keys,
    own_values,
    prefix_keys,
    prefix_values,
    passage_keys,
    passage_values,
    retrieval,
    location,
):
    grp, dev = lax.axis_index("grp"), lax.axis_index("dev")
    x, c, y, z = grp // NC, grp % NC, dev // NZ, dev % NZ
    low = y % 2

    def two_heads(cache):
        return lax.dynamic_slice(cache[0], (c * 256, x * 2 * D), (256, 2 * D))

    k2, v2 = two_heads(passage_keys), two_heads(passage_values)
    even = jnp.concatenate([k2[:, :D], v2[:, :D]], axis=1)
    odd = jnp.concatenate([k2[:, D:], v2[:, D:]], axis=1)
    kept = jnp.where(low == 0, even, odd)
    given = jnp.where(low == 0, odd, even)
    column = jnp.stack(
        [kept, send(given, y_by(1)), send(given, y_by(-1)), send(kept, y_by(2))]
    )
    column_ys = [y, y - 1, y + 1, y + 2]

    def by_head(rows, width):
        return rows.reshape(64, KV, width).transpose(1, 0, 2)

    def prefix_part(rows):
        return by_head(lax.dynamic_slice(rows, (low * 64, 0), (64, KV * D)), D)

    ids = jnp.zeros((RESP, T, D), jnp.bfloat16)
    ids = ids.at[:, :, :TOPK].set(retrieval.astype(jnp.bfloat16)[:, None, :])
    parcel = jnp.concatenate(
        [
            by_head(queries, GROUP * D),
            by_head(own_keys, D),
            by_head(own_values, D),
            prefix_part(prefix_keys),
            prefix_part(prefix_values),
            jnp.broadcast_to(ids.reshape(1, 64, D), (KV, 64, D)),
        ],
        axis=2,
    )
    got = lax.all_to_all(parcel, AXES, 0, 0, tiled=True, axis_index_groups=head_groups())
    theirs = send(got[:, :, 768:1024], other_core)

    chosen = got[:, :, 1024 : 1024 + TOPK].reshape(NR, T, TOPK)[:, 0].astype(jnp.int32)
    here = location[None, None, :] == jnp.arange(32)[:, None, None]
    at_place = jnp.sum(jnp.where(here, jnp.arange(32)[None, None, :], 0), axis=2)
    reads = jnp.any(chosen[None] == at_place[:, :, None], axis=2)
    ranks = jnp.sum(
        (reads[:, None, :] & (jnp.arange(NR)[None, :] < jnp.arange(NR)[:, None])[None]), axis=2
    )
    hit = reads[:, None, :] & (ranks[:, None, :] == jnp.arange(NR)[None, :, None])
    lists = jnp.sum(jnp.where(hit, jnp.arange(NR)[None, None, :] - NR, 0), axis=2) + NR
    lists = lists.astype(jnp.int32)
    counts_of = jnp.sum(reads, axis=1).astype(jnp.int32)

    q, acc, m = first_call(got, theirs)

    def places_of(offset, ys):
        return jnp.stack([(yy % NY) * NZ + (z + offset) % NZ for yy in ys]).astype(jnp.int32)

    def passages(chunks, acc, m, last=False):
        places = jnp.concatenate([places_of(offset, ys) for offset, ys, _ in chunks])
        pairs = [(block, send(block, other_core)) for _, _, block in chunks]
        return passage_call(places, counts_of, lists, q, acc, m, pairs, last)

    acc, m = passages([(0, column_ys, column)], acc, m)
    up = down = column
    for step in range(1, 4):
        up, down = send(up, z_by(1)), send(down, z_by(-1))
        acc, m = passages([(-step, column_ys, up), (step, column_ys, down)], acc, m)
    up, down = send(up[:2], z_by(1)), send(down[2:], z_by(-1))
    (out,) = passages([(4, column_ys[:2], up), (4, column_ys[2:], down)], acc, m, True)

    out = out.reshape(KV, 64, GROUP * D)
    home = lax.all_to_all(out, AXES, 0, 0, tiled=True, axis_index_groups=head_groups())
    return home.transpose(1, 0, 2).reshape(RESP, T, HEADS * D)


def solution(mesh):
    placed = (
        P(("grp", "dev"), None, None),
        P(("grp", "dev"), None, None),
        P(("grp", "dev"), None, None),
        P("grp", None),
        P("grp", None),
        P("dev", None, None),
        P("dev", None, None),
        P(("grp", "dev"), None),
        P(),
    )
    return jax.shard_map(
        per_device,
        mesh=mesh,
        in_specs=placed,
        out_specs=P(("grp", "dev"), None, None),
        check_vma=False,
    )
```

```python
import functools
import math

import jax
import jax.numpy as jnp
from jax import lax
from jax.experimental import pallas as pl
from jax.experimental.pallas import tpu as pltpu
from jax.sharding import PartitionSpec as P

HEADS = 32
KV = 8
D = 128
TOPK = 8
NX, NC, NY, NZ = 4, 2, 4, 8
AXES = ("grp", "dev")
RESP = 4
T = 16
GROUP = HEADS // KV
ROWS = GROUP * T
NR = 8 * RESP
SLOTS = NR + 1
BATCH = 8
PLACES = 32
COEF = math.log2(math.e) / math.sqrt(D)


def index_of(x, c, y, z):
    return ((x % NX) * NC + c) * (NY * NZ) + (y % NY) * NZ + z % NZ


def moves(to):
    places = [
        (x, c, y, z) for x in range(NX) for c in range(NC) for y in range(NY) for z in range(NZ)
    ]
    return [(index_of(*p), index_of(*to(*p))) for p in places]


def send(block, to):
    return lax.ppermute(block, AXES, moves(to))


def after(block, *earlier):
    return lax.optimization_barrier((block, *earlier))[0]


def y_by(step):
    return lambda x, c, y, z: (x, c, y + step, z)


def z_by(step):
    return lambda x, c, y, z: (x, c, y, z + step)


def other_core(x, c, y, z):
    return (x, 1 - c, y, z)


def head_groups():
    return [
        [index_of(x, c, 2 * high + low, z) for x in range(NX) for low in range(2)]
        for c in range(NC)
        for high in range(2)
        for z in range(NZ)
    ]


def any_turn(i):
    return jnp.where(i < 2, -i, i - 1)


def early_turn(i):
    return -i


def late_turn(i):
    return i + 1


def nt(a, b):
    return lax.dot_general(a, b, (((1,), (1,)), ((), ())), preferred_element_type=jnp.float32)


def parcel_kernel(
    low_ref, q_hbm, ok_hbm, ov_hbm, pk_hbm, pv_hbm, ids_ref, out_ref, q, ok, ov, pk, pv, sems
):
    rows = pl.ds(pl.multiple_of(low_ref[0] * 64, 64), 64)
    pairs = [(ok_hbm, ok), (ov_hbm, ov), (pk_hbm.at[rows, :], pk), (pv_hbm.at[rows, :], pv)]
    copies = [pltpu.make_async_copy(*pair, sems.at[k]) for k, pair in enumerate(pairs + [(q_hbm, q)])]
    for copy in copies:
        copy.start()
    for h in range(KV):
        out_ref[h, :, 1024:1152] = ids_ref[...]
    for k, source in enumerate((ok, ov, pk, pv)):
        copies[k].wait()
        for h in range(KV):
            out_ref[h, :, 512 + k * D : 512 + (k + 1) * D] = source[:, h * D : (h + 1) * D]
    copies[4].wait()
    for h in range(KV):
        out_ref[h, :, 0:512] = q[:, h * 512 : (h + 1) * 512]


def parcel_call(low, queries, own_keys, own_values, prefix_keys, prefix_values, ids):
    anywhere = pl.BlockSpec(memory_space=pl.ANY)
    vmem = pl.BlockSpec(memory_space=pltpu.VMEM)
    return pl.pallas_call(
        parcel_kernel,
        out_shape=jax.ShapeDtypeStruct((KV, 64, 1152), jnp.bfloat16),
        in_specs=[pl.BlockSpec(memory_space=pltpu.SMEM)] + [anywhere] * 5 + [vmem],
        out_specs=vmem,
        scratch_shapes=[pltpu.VMEM((64, HEADS * D), jnp.bfloat16)]
        + [pltpu.VMEM((64, KV * D), jnp.bfloat16)] * 4
        + [pltpu.SemaphoreType.DMA((5,))],
        compiler_params=pltpu.CompilerParams(vmem_limit_bytes=8 * 1024 * 1024),
        cost_estimate=pl.CostEstimate(flops=0, bytes_accessed=6 * 1024 * 1024, transcendentals=0),
        name="parcel",
    )(
        low.reshape(1),
        queries.reshape(64, HEADS * D),
        own_keys.reshape(64, KV * D),
        own_values.reshape(64, KV * D),
        prefix_keys,
        prefix_values,
        ids,
    )


def first_kernel(
    ids_ref, at_ref, got_ref, theirs_ref, q_ref, acc_ref, m_ref, count_ref, list_ref, keys, values
):
    for s in range(8):
        at = pl.ds(s * 64, 64)
        keys[at, :] = got_ref[s, :, 768:896]
        values[at, 0:D] = got_ref[s, :, 896:1024]
        at = pl.ds(512 + s * 64, 64)
        keys[at, :] = theirs_ref[s, :, 0:D]
        values[at, 0:D] = theirs_ref[s, :, D : 2 * D]
    values[:, D:] = jnp.ones((1024, D), jnp.bfloat16)
    q_ref[NR * ROWS :, :] = jnp.zeros((ROWS, D), jnp.bfloat16)
    m_ref[NR * ROWS :, :] = jnp.zeros((ROWS, D), jnp.float32)
    acc_ref[NR * ROWS :, :] = jnp.zeros((ROWS, 2 * D), jnp.float32)
    for p in range(PLACES + 1):
        count_ref[p] = 0
    row = lax.broadcasted_iota(jnp.int32, (RESP * ROWS, RESP * T), 0)
    col = lax.broadcasted_iota(jnp.int32, (RESP * ROWS, RESP * T), 1)
    seen = (row // ROWS == col // T) & (row % T >= col % T)

    @pl.loop(0, 4)
    def _(pair):
        for k in range(8 * TOPK):
            r = pair * 8 + k // TOPK
            place = at_ref[ids_ref[r, k % TOPK]]
            rank = count_ref[place]
            list_ref[place, rank] = r
            count_ref[place] = rank + 1
        two = [pair * 2, pair * 2 + 1]
        q = [
            jnp.concatenate(
                [
                    got_ref[s, a * T : (a + 1) * T, g * D : (g + 1) * D]
                    for a in range(RESP)
                    for g in range(GROUP)
                ],
                axis=0,
            )
            for s in two
        ]
        own = [
            jnp.where(seen, nt(q[i], got_ref[s, :, 512:640]), -jnp.inf) for i, s in enumerate(two)
        ]
        far = [nt(q[i], keys[...]) for i in range(2)]
        m = []
        for i in range(2):
            top = jnp.maximum(
                jnp.max(far[i], axis=1, keepdims=True), jnp.max(own[i], axis=1, keepdims=True)
            )
            m.append(jnp.broadcast_to(top * COEF, (RESP * ROWS, D)))
        for i, s in enumerate(two):
            at = pl.ds(pl.multiple_of(s * (RESP * ROWS), RESP * ROWS), RESP * ROWS)
            p = jnp.concatenate(
                [
                    jnp.exp2(far[i][:, j * D : (j + 1) * D] * COEF - m[i]).astype(jnp.bfloat16)
                    for j in range(8)
                ],
                axis=1,
            )
            po = jnp.exp2(own[i] * COEF - m[i][:, : RESP * T]).astype(jnp.bfloat16)
            vo = jnp.concatenate(
                [got_ref[s, :, 640:768], jnp.ones((RESP * T, D), jnp.bfloat16)], axis=1
            )
            acc = jnp.dot(p, values[...], preferred_element_type=jnp.float32)
            q_ref[at, :] = q[i]
            m_ref[at, :] = m[i]
            acc_ref[at, :] = acc + jnp.dot(po, vo, preferred_element_type=jnp.float32)


def first_call(ids, location, got, theirs):
    n = SLOTS * ROWS
    vmem = pl.BlockSpec(memory_space=pltpu.VMEM)
    smem = pl.BlockSpec(memory_space=pltpu.SMEM)
    return pl.pallas_call(
        first_kernel,
        out_shape=(
            jax.ShapeDtypeStruct((n, D), jnp.bfloat16),
            jax.ShapeDtypeStruct((n, 2 * D), jnp.float32),
            jax.ShapeDtypeStruct((n, D), jnp.float32),
            jax.ShapeDtypeStruct((PLACES + 1,), jnp.int32),
            jax.ShapeDtypeStruct((PLACES + 1, NR), jnp.int32),
        ),
        in_specs=[smem] * 2 + [vmem] * 2,
        out_specs=(vmem,) * 3 + (smem,) * 2,
        scratch_shapes=[
            pltpu.VMEM((1024, D), jnp.bfloat16),
            pltpu.VMEM((1024, 2 * D), jnp.bfloat16),
        ],
        compiler_params=pltpu.CompilerParams(vmem_limit_bytes=16 * 1024 * 1024),
        cost_estimate=pl.CostEstimate(
            flops=8 * 2048 * 1088 * D, bytes_accessed=6 * 1024 * 1024, transcendentals=2048 * 1088
        ),
        name="prefix_and_own",
    )(ids, location, got, theirs)


def passage_kernel(steps, counts, last, spot_ref, count_ref, list_ref, q_ref, acc_in, m_in, *rest):
    blocks = rest[:4]
    if last:
        out_ref, acc, m = rest[4:]
    else:
        acc, m = rest[4:]
    acc[...] = acc_in[...]
    m[...] = m_in[...]
    ones = jnp.ones((256, D), jnp.bfloat16)

    def place_of(s, i):
        turn = steps[s][1](i)
        return ((spot_ref[0] + turn) & (NY - 1)) * NZ + ((spot_ref[1] + steps[s][0]) & (NZ - 1))

    def batches(s):
        total = 0
        for i in range(counts[s]):
            count = count_ref[place_of(s, i)]
            total = total + jnp.maximum((count + BATCH - 1) // BATCH, 1)
        return total

    def step(_, carry):
        at, sc, keep = [], [], []
        ahead = []
        for s, (i, b) in enumerate(carry):
            i_here = jnp.minimum(i, counts[s] - 1)
            place = jnp.where(i < counts[s], place_of(s, i_here), PLACES)
            count = count_ref[place]
            rows = [
                jnp.where(b * BATCH + k < count, list_ref[place, b * BATCH + k], NR)
                for k in range(BATCH)
            ]
            at.append([pl.ds(pl.multiple_of(r * ROWS, ROWS), ROWS) for r in rows])
            full = (b + 1) * BATCH >= count
            ahead.append((i + full.astype(jnp.int32), jnp.where(full, 0, b + 1)))
            q = jnp.concatenate([q_ref[a, :] for a in at[s]], axis=0)
            here = [blocks[2 * s], blocks[2 * s + 1]]
            sc.append([nt(q, h[i_here, :, 0:D]) for h in here])
            keep.append([jnp.concatenate([h[i_here, :, D:], ones], axis=1) for h in here])
        new, shrink = [], []
        for s in range(2):
            top = jnp.maximum(
                jnp.max(sc[s][0], axis=1, keepdims=True), jnp.max(sc[s][1], axis=1, keepdims=True)
            )
            old = jnp.concatenate([m[a, :] for a in at[s]], axis=0)
            new.append(jnp.maximum(old, top * COEF))
            shrink.append(jnp.exp2(old - new[s]))
            for k, a in enumerate(at[s]):
                m[a, :] = new[s][k * ROWS : (k + 1) * ROWS]
        mixed = []
        for s in range(2):
            mixed.append(0)
            for h in range(2):
                p = jnp.concatenate(
                    [
                        jnp.exp2(sc[s][h][:, j * D : (j + 1) * D] * COEF - new[s]).astype(
                            jnp.bfloat16
                        )
                        for j in range(2)
                    ],
                    axis=1,
                )
                mixed[s] = mixed[s] + jnp.dot(p, keep[s][h], preferred_element_type=jnp.float32)
        for s in range(2):
            for k, a in enumerate(at[s]):
                part = slice(k * ROWS, (k + 1) * ROWS)
                acc[a, 0:D] = acc[a, 0:D] * shrink[s][part] + mixed[s][part, 0:D]
                acc[a, D:] = acc[a, D:] * shrink[s][part] + mixed[s][part, D:]
        return tuple(ahead)

    start = ((jnp.int32(0), jnp.int32(0)),) * 2
    lax.fori_loop(0, jnp.maximum(batches(0), batches(1)), step, start)
    if last:

        @pl.loop(0, NR)
        def _(r):
            at = pl.ds(pl.multiple_of(r * ROWS, ROWS), ROWS)
            o = (acc[at, 0:D] / acc[at, D:]).astype(jnp.bfloat16)
            for g in range(GROUP):
                out_ref[pl.ds(pl.multiple_of(r * T, T), T), g * D : (g + 1) * D] = o[
                    g * T : (g + 1) * T
                ]


def passage_call(spot, counts_of, lists, q, acc, m, steps, pairs, last):
    n = SLOTS * ROWS
    counts = tuple(mine.shape[0] for mine, _ in pairs)
    total = sum(counts)
    state = (jax.ShapeDtypeStruct((n, 2 * D), jnp.float32), jax.ShapeDtypeStruct((n, D), jnp.float32))
    scratch = []
    if last:
        out_shape = (jax.ShapeDtypeStruct((NR * T, GROUP * D), jnp.bfloat16),)
        scratch = [pltpu.VMEM((n, 2 * D), jnp.float32), pltpu.VMEM((n, D), jnp.float32)]
        aliases = {}
    else:
        out_shape = state
        aliases = {4: 0, 5: 1}
    vmem = pl.BlockSpec(memory_space=pltpu.VMEM)
    smem = pl.BlockSpec(memory_space=pltpu.SMEM)
    return pl.pallas_call(
        functools.partial(passage_kernel, steps, counts, last),
        out_shape=out_shape,
        in_specs=[smem] * 3 + [vmem] * (3 + 2 * len(counts)),
        out_specs=(vmem,) * len(out_shape),
        scratch_shapes=scratch,
        input_output_aliases=aliases,
        compiler_params=pltpu.CompilerParams(vmem_limit_bytes=20 * 1024 * 1024),
        cost_estimate=pl.CostEstimate(
            flops=16 * total * 10 * ROWS * 512 * D,
            bytes_accessed=6 * 1024 * 1024,
            transcendentals=total * 10 * ROWS * 512,
        ),
        name="passages",
    )(spot, counts_of, lists, q, acc, m, *[a for pair in pairs for a in pair])


def per_device(
    queries,
    own_keys,
    own_values,
    prefix_keys,
    prefix_values,
    passage_keys,
    passage_values,
    retrieval,
    location,
):
    grp, dev = lax.axis_index("grp"), lax.axis_index("dev")
    x, c, y, z = grp >> 1, grp & 1, dev >> 3, dev & 7
    low = y & 1
    spot = jnp.stack([y, z])

    def two_heads(cache):
        return lax.dynamic_slice(cache[0], (c * 256, x * 2 * D), (256, 2 * D))

    k2, v2 = two_heads(passage_keys), two_heads(passage_values)
    even = jnp.concatenate([k2[:, :D], v2[:, :D]], axis=1)
    odd = jnp.concatenate([k2[:, D:], v2[:, D:]], axis=1)
    kept = jnp.where(low == 0, even, odd)
    given = jnp.where(low == 0, odd, even)
    column = jnp.stack(
        [kept, send(given, y_by(1)), send(given, y_by(-1)), send(kept, y_by(2))]
    )

    ids = jnp.pad(retrieval.astype(jnp.bfloat16), ((0, 0), (0, D - TOPK)))
    ids = jnp.broadcast_to(ids[:, None, :], (RESP, T, D)).reshape(64, D)
    parcel = parcel_call(after(low, given), queries, own_keys, own_values, prefix_keys, prefix_values, ids)
    got = lax.all_to_all(after(parcel, column), AXES, 0, 0, tiled=True, axis_index_groups=head_groups())
    theirs = send(got[:, :, 768:1024], other_core)
    chosen = got[:, :, 1024 : 1024 + TOPK].reshape(NR, T, TOPK)[:, 0].astype(jnp.int32)
    q, acc, m, counts_of, lists = first_call(chosen, location, got, theirs)

    def passages(chunks, acc, m, last=False):
        steps = tuple((offset, turn) for offset, turn, _ in chunks)
        pairs = [pair for _, _, pair in chunks]
        return passage_call(spot, counts_of, lists, q, acc, m, steps, pairs, last)

    def swap(block):
        return block, send(block, other_core)

    first = [swap(column[:2]), swap(column[2:])]
    up1, down1 = send(column, z_by(1)), send(column, z_by(-1))
    ups, downs = [swap(up1)], [swap(down1)]
    swapped = (first[0][1], first[1][1])
    ups.append(swap(send(after(up1, *swapped), z_by(1))))
    downs.append(swap(send(after(down1, *swapped), z_by(-1))))
    swapped = (ups[0][1], downs[0][1])
    ups.append(swap(send(after(ups[1][0], m, *swapped), z_by(1))))
    acc, m = passages([(0, early_turn, first[0]), (0, late_turn, first[1])], acc, m)
    downs.append(swap(send(after(downs[1][0], m, *swapped), z_by(-1))))
    for k in range(2):
        acc, m = passages([(-k - 1, any_turn, ups[k]), (k + 1, any_turn, downs[k])], acc, m)
    swapped = (ups[1][1], downs[1][1])
    last_up = swap(send(after(ups[2][0], m, *swapped)[:2], z_by(1)))
    last_down = swap(send(after(downs[2][0], m, *swapped)[2:], z_by(-1)))
    acc, m = passages([(-3, any_turn, ups[2]), (3, any_turn, downs[2])], acc, m)
    (out,) = passages([(4, early_turn, last_up), (4, late_turn, last_down)], acc, m, True)

    out = out.reshape(KV, 64, GROUP * D)
    home = lax.all_to_all(out, AXES, 0, 0, tiled=True, axis_index_groups=head_groups())
    return home.transpose(1, 0, 2).reshape(RESP, T, HEADS * D)


def solution(mesh):
    placed = (
        P(("grp", "dev"), None, None),
        P(("grp", "dev"), None, None),
        P(("grp", "dev"), None, None),
        P("grp", None),
        P("grp", None),
        P("dev", None, None),
        P("dev", None, None),
        P(("grp", "dev"), None),
        P(),
    )
    return jax.shard_map(
        per_device,
        mesh=mesh,
        in_specs=placed,
        out_specs=P(("grp", "dev"), None, None),
        check_vma=False,
    )
```

```python
import functools
import math
import typing

import jax
import jax.numpy as jnp
from jax import lax
from jax.experimental import pallas as pl
from jax.experimental.pallas import tpu as pltpu
from jax.sharding import PartitionSpec as P

HEADS = 32
KV = 8
D = 128
TOPK = 8
NX, NC, NY, NZ = 4, 2, 4, 8
AXES = ("grp", "dev")
RESP = 4
T = 16
GROUP = HEADS // KV
ROWS = GROUP * T
NR = 8 * RESP
SLOTS = NR + 1
BATCH = 8
PLACES = 32
COEF = math.log2(math.e) / math.sqrt(D)


def index_of(x, c, y, z):
    return ((x % NX) * NC + c) * (NY * NZ) + (y % NY) * NZ + z % NZ


def moves(to):
    places = [
        (x, c, y, z) for x in range(NX) for c in range(NC) for y in range(NY) for z in range(NZ)
    ]
    return [(index_of(*p), index_of(*to(*p))) for p in places]


def send(block, to):
    return lax.ppermute(block, AXES, moves(to))


def after(block, *earlier):
    return lax.optimization_barrier((block, *earlier))[0]


def y_by(step):
    return lambda x, c, y, z: (x, c, y + step, z)


def z_by(step):
    return lambda x, c, y, z: (x, c, y, z + step)


def other_core(x, c, y, z):
    return (x, 1 - c, y, z)


def head_groups():
    return [
        [index_of(x, c, 2 * high + low, z) for x in range(NX) for low in range(2)]
        for c in range(NC)
        for high in range(2)
        for z in range(NZ)
    ]


class Stream(typing.NamedTuple):
    pair: int
    base: int
    count: int
    offset: int


def any_turn(i):
    return jnp.where(i < 2, -i, i - 1)


def split(pair, offset):
    return (Stream(pair, 0, 2, offset), Stream(pair, 2, 2, offset))


def both(pair, offset):
    return (Stream(pair, 0, 4, -offset), Stream(pair + 1, 0, 4, offset))


def nt(a, b):
    return lax.dot_general(a, b, (((1,), (1,)), ((), ())), preferred_element_type=jnp.float32)


def parcel_kernel(
    low_ref, q_hbm, ok_hbm, ov_hbm, pk_hbm, pv_hbm, ids_ref, out_ref, q, ok, ov, pk, pv, sems
):
    rows = pl.ds(pl.multiple_of(low_ref[0] * 64, 64), 64)
    pairs = [(ok_hbm, ok), (ov_hbm, ov), (pk_hbm.at[rows, :], pk), (pv_hbm.at[rows, :], pv)]
    copies = [pltpu.make_async_copy(*pair, sems.at[k]) for k, pair in enumerate(pairs + [(q_hbm, q)])]
    for copy in copies:
        copy.start()
    for h in range(KV):
        out_ref[h, :, 1024:1152] = ids_ref[...]
    for k, source in enumerate((ok, ov, pk, pv)):
        copies[k].wait()
        for h in range(KV):
            out_ref[h, :, 512 + k * D : 512 + (k + 1) * D] = source[:, h * D : (h + 1) * D]
    copies[4].wait()
    for h in range(KV):
        out_ref[h, :, 0:512] = q[:, h * 512 : (h + 1) * 512]


def parcel_call(low, queries, own_keys, own_values, prefix_keys, prefix_values, ids):
    anywhere = pl.BlockSpec(memory_space=pl.ANY)
    vmem = pl.BlockSpec(memory_space=pltpu.VMEM)
    return pl.pallas_call(
        parcel_kernel,
        out_shape=jax.ShapeDtypeStruct((KV, 64, 1152), jnp.bfloat16),
        in_specs=[pl.BlockSpec(memory_space=pltpu.SMEM)] + [anywhere] * 5 + [vmem],
        out_specs=vmem,
        scratch_shapes=[pltpu.VMEM((64, HEADS * D), jnp.bfloat16)]
        + [pltpu.VMEM((64, KV * D), jnp.bfloat16)] * 4
        + [pltpu.SemaphoreType.DMA((5,))],
        compiler_params=pltpu.CompilerParams(vmem_limit_bytes=8 * 1024 * 1024),
        cost_estimate=pl.CostEstimate(flops=0, bytes_accessed=6 * 1024 * 1024, transcendentals=0),
        name="parcel",
    )(
        low.reshape(1),
        queries.reshape(64, HEADS * D),
        own_keys.reshape(64, KV * D),
        own_values.reshape(64, KV * D),
        prefix_keys,
        prefix_values,
        ids,
    )


def first_kernel(
    ids_ref, at_ref, got_ref, theirs_ref, q_ref, acc_ref, m_ref, count_ref, list_ref, keys, values
):
    for s in range(8):
        at = pl.ds(s * 64, 64)
        keys[at, :] = got_ref[s, :, 768:896]
        values[at, 0:D] = got_ref[s, :, 896:1024]
        at = pl.ds(512 + s * 64, 64)
        keys[at, :] = theirs_ref[s, :, 0:D]
        values[at, 0:D] = theirs_ref[s, :, D : 2 * D]
    values[:, D:] = jnp.ones((1024, D), jnp.bfloat16)
    q_ref[NR * ROWS :, :] = jnp.zeros((ROWS, D), jnp.bfloat16)
    m_ref[NR * ROWS :, :] = jnp.zeros((ROWS, D), jnp.float32)
    acc_ref[NR * ROWS :, :] = jnp.zeros((ROWS, 2 * D), jnp.float32)
    for p in range(PLACES + 1):
        count_ref[p] = 0
    row = lax.broadcasted_iota(jnp.int32, (RESP * ROWS, RESP * T), 0)
    col = lax.broadcasted_iota(jnp.int32, (RESP * ROWS, RESP * T), 1)
    seen = (row // ROWS == col // T) & (row % T >= col % T)

    @pl.loop(0, 4)
    def _(pair):
        for k in range(8 * TOPK):
            r = pair * 8 + k // TOPK
            place = at_ref[ids_ref[r, k % TOPK]]
            rank = count_ref[place]
            list_ref[place, rank] = r
            count_ref[place] = rank + 1
        two = [pair * 2, pair * 2 + 1]
        q = [
            jnp.concatenate(
                [
                    got_ref[s, a * T : (a + 1) * T, g * D : (g + 1) * D]
                    for a in range(RESP)
                    for g in range(GROUP)
                ],
                axis=0,
            )
            for s in two
        ]
        own = [
            jnp.where(seen, nt(q[i], got_ref[s, :, 512:640]), -jnp.inf) for i, s in enumerate(two)
        ]
        far = [nt(q[i], keys[...]) for i in range(2)]
        m = []
        for i in range(2):
            top = jnp.maximum(
                jnp.max(far[i], axis=1, keepdims=True), jnp.max(own[i], axis=1, keepdims=True)
            )
            m.append(jnp.broadcast_to(top * COEF, (RESP * ROWS, D)))
        for i, s in enumerate(two):
            at = pl.ds(pl.multiple_of(s * (RESP * ROWS), RESP * ROWS), RESP * ROWS)
            p = jnp.concatenate(
                [
                    jnp.exp2(far[i][:, j * D : (j + 1) * D] * COEF - m[i]).astype(jnp.bfloat16)
                    for j in range(8)
                ],
                axis=1,
            )
            po = jnp.exp2(own[i] * COEF - m[i][:, : RESP * T]).astype(jnp.bfloat16)
            vo = jnp.concatenate(
                [got_ref[s, :, 640:768], jnp.ones((RESP * T, D), jnp.bfloat16)], axis=1
            )
            acc = jnp.dot(p, values[...], preferred_element_type=jnp.float32)
            q_ref[at, :] = q[i]
            m_ref[at, :] = m[i]
            acc_ref[at, :] = acc + jnp.dot(po, vo, preferred_element_type=jnp.float32)


def first_call(ids, location, got, theirs):
    n = SLOTS * ROWS
    vmem = pl.BlockSpec(memory_space=pltpu.VMEM)
    smem = pl.BlockSpec(memory_space=pltpu.SMEM)
    return pl.pallas_call(
        first_kernel,
        out_shape=(
            jax.ShapeDtypeStruct((n, D), jnp.bfloat16),
            jax.ShapeDtypeStruct((n, 2 * D), jnp.float32),
            jax.ShapeDtypeStruct((n, D), jnp.float32),
            jax.ShapeDtypeStruct((PLACES + 1,), jnp.int32),
            jax.ShapeDtypeStruct((PLACES + 1, NR), jnp.int32),
        ),
        in_specs=[smem] * 2 + [vmem] * 2,
        out_specs=(vmem,) * 3 + (smem,) * 2,
        scratch_shapes=[
            pltpu.VMEM((1024, D), jnp.bfloat16),
            pltpu.VMEM((1024, 2 * D), jnp.bfloat16),
        ],
        compiler_params=pltpu.CompilerParams(vmem_limit_bytes=16 * 1024 * 1024),
        cost_estimate=pl.CostEstimate(
            flops=8 * 2048 * 1088 * D, bytes_accessed=6 * 1024 * 1024, transcendentals=2048 * 1088
        ),
        name="prefix_and_own",
    )(ids, location, got, theirs)


def passage_kernel(rounds, n_pairs, last, spot_ref, count_ref, list_ref, q_ref, acc_in, m_in, *rest):
    blocks = rest[: 2 * n_pairs]
    if last:
        out_ref, acc, m = rest[2 * n_pairs :]
    else:
        acc, m = rest[2 * n_pairs :]
    acc[...] = acc_in[...]
    m[...] = m_in[...]
    ones = jnp.ones((256, D), jnp.bfloat16)

    for streams in rounds:
        run_streams(streams, blocks, ones, spot_ref, count_ref, list_ref, q_ref, acc, m)
    if last:

        @pl.loop(0, NR)
        def _(r):
            at = pl.ds(pl.multiple_of(r * ROWS, ROWS), ROWS)
            o = (acc[at, 0:D] / acc[at, D:]).astype(jnp.bfloat16)
            for g in range(GROUP):
                out_ref[pl.ds(pl.multiple_of(r * T, T), T), g * D : (g + 1) * D] = o[
                    g * T : (g + 1) * T
                ]


def run_streams(streams, blocks, ones, spot_ref, count_ref, list_ref, q_ref, acc, m):
    def place_of(s, i):
        turn = any_turn(streams[s].base + i)
        up = spot_ref[1] + streams[s].offset
        return ((spot_ref[0] + turn) & (NY - 1)) * NZ + (up & (NZ - 1))

    def batches(s):
        total = 0
        for i in range(streams[s].count):
            total = total + jnp.maximum((count_ref[place_of(s, i)] + BATCH - 1) // BATCH, 1)
        return total

    def step(_, carry):
        at, sc, keep = [], [], []
        ahead = []
        for s, (i, b) in enumerate(carry):
            i_here = jnp.minimum(i, streams[s].count - 1)
            place = jnp.where(i < streams[s].count, place_of(s, i_here), PLACES)
            count = count_ref[place]
            rows = [
                jnp.where(b * BATCH + k < count, list_ref[place, b * BATCH + k], NR)
                for k in range(BATCH)
            ]
            at.append([pl.ds(pl.multiple_of(r * ROWS, ROWS), ROWS) for r in rows])
            full = (b + 1) * BATCH >= count
            ahead.append((i + full.astype(jnp.int32), jnp.where(full, 0, b + 1)))
            q = jnp.concatenate([q_ref[a, :] for a in at[s]], axis=0)
            pair = streams[s].pair
            here = [h.at[streams[s].base + i_here] for h in blocks[2 * pair : 2 * pair + 2]]
            sc.append([nt(q, h[:, 0:D]) for h in here])
            keep.append([jnp.concatenate([h[:, D:], ones], axis=1) for h in here])
        new, shrink = [], []
        for s in range(2):
            top = jnp.maximum(
                jnp.max(sc[s][0], axis=1, keepdims=True), jnp.max(sc[s][1], axis=1, keepdims=True)
            )
            old = jnp.concatenate([m[a, :] for a in at[s]], axis=0)
            new.append(jnp.maximum(old, top * COEF))
            shrink.append(jnp.exp2(old - new[s]))
            for k, a in enumerate(at[s]):
                m[a, :] = new[s][k * ROWS : (k + 1) * ROWS]
        mixed = []
        for s in range(2):
            mixed.append(0)
            for h in range(2):
                p = jnp.concatenate(
                    [
                        jnp.exp2(sc[s][h][:, j * D : (j + 1) * D] * COEF - new[s]).astype(
                            jnp.bfloat16
                        )
                        for j in range(2)
                    ],
                    axis=1,
                )
                mixed[s] = mixed[s] + jnp.dot(p, keep[s][h], preferred_element_type=jnp.float32)
        for s in range(2):
            for k, a in enumerate(at[s]):
                part = slice(k * ROWS, (k + 1) * ROWS)
                acc[a, 0:D] = acc[a, 0:D] * shrink[s][part] + mixed[s][part, 0:D]
                acc[a, D:] = acc[a, D:] * shrink[s][part] + mixed[s][part, D:]
        return tuple(ahead)

    start = ((jnp.int32(0), jnp.int32(0)),) * 2
    lax.fori_loop(0, jnp.maximum(batches(0), batches(1)), step, start)


def passage_call(spot, counts_of, lists, q, acc, m, rounds, pairs, last=False):
    n = SLOTS * ROWS
    total = sum(stream.count for streams in rounds for stream in streams)
    state = (jax.ShapeDtypeStruct((n, 2 * D), jnp.float32), jax.ShapeDtypeStruct((n, D), jnp.float32))
    scratch = []
    if last:
        out_shape = (jax.ShapeDtypeStruct((NR * T, GROUP * D), jnp.bfloat16),)
        scratch = [pltpu.VMEM((n, 2 * D), jnp.float32), pltpu.VMEM((n, D), jnp.float32)]
        aliases = {}
    else:
        out_shape = state
        aliases = {4: 0, 5: 1}
    vmem = pl.BlockSpec(memory_space=pltpu.VMEM)
    smem = pl.BlockSpec(memory_space=pltpu.SMEM)
    return pl.pallas_call(
        functools.partial(passage_kernel, rounds, len(pairs), last),
        out_shape=out_shape,
        in_specs=[smem] * 3 + [vmem] * (3 + 2 * len(pairs)),
        out_specs=(vmem,) * len(out_shape),
        scratch_shapes=scratch,
        input_output_aliases=aliases,
        compiler_params=pltpu.CompilerParams(vmem_limit_bytes=20 * 1024 * 1024),
        cost_estimate=pl.CostEstimate(
            flops=16 * total * 10 * ROWS * 512 * D,
            bytes_accessed=6 * 1024 * 1024,
            transcendentals=total * 10 * ROWS * 512,
        ),
        name="passages",
    )(spot, counts_of, lists, q, acc, m, *[a for pair in pairs for a in pair])


def per_device(
    queries,
    own_keys,
    own_values,
    prefix_keys,
    prefix_values,
    passage_keys,
    passage_values,
    retrieval,
    location,
):
    grp, dev = lax.axis_index("grp"), lax.axis_index("dev")
    x, c, y, z = grp >> 1, grp & 1, dev >> 3, dev & 7
    low = y & 1
    spot = jnp.stack([y, z])

    def two_heads(cache):
        return lax.dynamic_slice(cache[0], (c * 256, x * 2 * D), (256, 2 * D))

    k2, v2 = two_heads(passage_keys), two_heads(passage_values)
    even = jnp.concatenate([k2[:, :D], v2[:, :D]], axis=1)
    odd = jnp.concatenate([k2[:, D:], v2[:, D:]], axis=1)
    kept = jnp.where(low == 0, even, odd)
    given = jnp.where(low == 0, odd, even)
    ids = jnp.pad(retrieval.astype(jnp.bfloat16), ((0, 0), (0, D - TOPK)))
    ids = jnp.broadcast_to(ids[:, None, :], (RESP, T, D)).reshape(64, D)
    parcel = parcel_call(after(low, given), queries, own_keys, own_values, prefix_keys, prefix_values, ids)
    pieces = [kept, send(given, y_by(1)), send(given, y_by(-1)), send(kept, y_by(2))]
    pieces[3] = after(pieces[3], parcel)
    column = jnp.stack(pieces)
    def swap(block):
        return block, send(block, other_core)

    got = lax.all_to_all(after(parcel, column), AXES, 0, 0, tiled=True, axis_index_groups=head_groups())
    up1, down1 = send(column, z_by(1)), send(column, z_by(-1))
    up2, down2 = send(up1, z_by(1)), send(down1, z_by(-1))
    one = [swap(up1), swap(down1)]
    got = after(got, one[0][1], one[1][1])
    here = swap(after(column, got))
    theirs = send(got[:, :, 768:1024], other_core)
    chosen = got[:, :, 1024 : 1024 + TOPK].reshape(NR, T, TOPK)[:, 0].astype(jnp.int32)
    q, acc, m, counts_of, lists = first_call(chosen, location, got, theirs)

    state = (spot, counts_of, lists, q)
    seen = (m, one[0][1], one[1][1])
    up3, down3 = send(after(up2, *seen), z_by(1)), send(after(down2, *seen), z_by(-1))
    two = [swap(after(up2, m)), swap(after(down2, m))]
    acc, m = passage_call(*state, acc, m, (split(0, 0), both(1, 1)), [here] + one)
    up3, down3 = after(up3, m), after(down3, m)
    four = send(jnp.where(c == 0, up3, down3), lambda x, c, y, z: (x, c, y, z + 1 - 2 * c))
    three = [swap(up3), swap(down3)]
    acc, m = passage_call(*state, acc, m, (both(0, 2),), two)
    four = after(four, m)
    acc, m = passage_call(*state, acc, m, (both(0, 3),), three)
    (out,) = passage_call(*state, acc, m, (split(0, 4),), [swap(four)], True)

    out = out.reshape(KV, 64, GROUP * D)
    home = lax.all_to_all(out, AXES, 0, 0, tiled=True, axis_index_groups=head_groups())
    return home.transpose(1, 0, 2).reshape(RESP, T, HEADS * D)


def solution(mesh):
    placed = (
        P(("grp", "dev"), None, None),
        P(("grp", "dev"), None, None),
        P(("grp", "dev"), None, None),
        P("grp", None),
        P("grp", None),
        P("dev", None, None),
        P("dev", None, None),
        P(("grp", "dev"), None),
        P(),
    )
    return jax.shard_map(
        per_device,
        mesh=mesh,
        in_specs=placed,
        out_specs=P(("grp", "dev"), None, None),
        check_vma=False,
    )
```

```python
import functools
import math
import typing

import jax
import jax.numpy as jnp
from jax import lax
from jax.experimental import pallas as pl
from jax.experimental.pallas import tpu as pltpu
from jax.sharding import PartitionSpec as P

HEADS = 32
KV = 8
D = 128
TOPK = 8
NX, NC, NY, NZ = 4, 2, 4, 8
AXES = ("grp", "dev")
RESP = 4
T = 16
GROUP = HEADS // KV
ROWS = GROUP * T
NR = 8 * RESP
SLOTS = NR + 1
BATCH = 8
PLACES = 32
COEF = math.log2(math.e) / math.sqrt(D)


def index_of(x, c, y, z):
    return ((x % NX) * NC + c) * (NY * NZ) + (y % NY) * NZ + z % NZ


def moves(to):
    places = [
        (x, c, y, z) for x in range(NX) for c in range(NC) for y in range(NY) for z in range(NZ)
    ]
    return [(index_of(*p), index_of(*to(*p))) for p in places]


def send(block, to):
    return lax.ppermute(block, AXES, moves(to))


def after(block, *earlier):
    return lax.optimization_barrier((block, *earlier))[0]


def y_by(step):
    return lambda x, c, y, z: (x, c, y + step, z)


def z_by(step):
    return lambda x, c, y, z: (x, c, y, z + step)


def other_core(x, c, y, z):
    return (x, 1 - c, y, z)


def head_groups():
    return [
        [index_of(x, c, 2 * high + low, z) for x in range(NX) for low in range(2)]
        for c in range(NC)
        for high in range(2)
        for z in range(NZ)
    ]


class Stream(typing.NamedTuple):
    pair: int
    base: int
    count: int
    offset: int


def any_turn(i):
    return jnp.where(i < 2, -i, i - 1)


def split(pair, offset):
    return (Stream(pair, 0, 2, offset), Stream(pair, 2, 2, offset))


def both(pair, offset):
    return (Stream(pair, 0, 4, -offset), Stream(pair + 1, 0, 4, offset))


def nt(a, b):
    return lax.dot_general(a, b, (((1,), (1,)), ((), ())), preferred_element_type=jnp.float32)


def parcel_kernel(
    low_ref, q_hbm, ok_hbm, ov_hbm, pk_hbm, pv_hbm, ids_ref, out_ref, q, ok, ov, pk, pv, sems
):
    rows = pl.ds(pl.multiple_of(low_ref[0] * 64, 64), 64)
    pairs = [(ok_hbm, ok), (ov_hbm, ov), (pk_hbm.at[rows, :], pk), (pv_hbm.at[rows, :], pv)]
    copies = [pltpu.make_async_copy(*pair, sems.at[k]) for k, pair in enumerate(pairs + [(q_hbm, q)])]
    for copy in copies:
        copy.start()
    for h in range(KV):
        out_ref[h, :, 1024:1152] = ids_ref[...]
    for k, source in enumerate((ok, ov, pk, pv)):
        copies[k].wait()
        for h in range(KV):
            out_ref[h, :, 512 + k * D : 512 + (k + 1) * D] = source[:, h * D : (h + 1) * D]
    copies[4].wait()
    for h in range(KV):
        out_ref[h, :, 0:512] = q[:, h * 512 : (h + 1) * 512]


def parcel_call(low, queries, own_keys, own_values, prefix_keys, prefix_values, ids):
    anywhere = pl.BlockSpec(memory_space=pl.ANY)
    vmem = pl.BlockSpec(memory_space=pltpu.VMEM)
    return pl.pallas_call(
        parcel_kernel,
        out_shape=jax.ShapeDtypeStruct((KV, 64, 1152), jnp.bfloat16),
        in_specs=[pl.BlockSpec(memory_space=pltpu.SMEM)] + [anywhere] * 5 + [vmem],
        out_specs=vmem,
        scratch_shapes=[pltpu.VMEM((64, HEADS * D), jnp.bfloat16)]
        + [pltpu.VMEM((64, KV * D), jnp.bfloat16)] * 4
        + [pltpu.SemaphoreType.DMA((5,))],
        compiler_params=pltpu.CompilerParams(vmem_limit_bytes=8 * 1024 * 1024),
        cost_estimate=pl.CostEstimate(flops=0, bytes_accessed=6 * 1024 * 1024, transcendentals=0),
        name="parcel",
    )(
        low.reshape(1),
        queries.reshape(64, HEADS * D),
        own_keys.reshape(64, KV * D),
        own_values.reshape(64, KV * D),
        prefix_keys,
        prefix_values,
        ids,
    )


def first_kernel(
    ids_ref, at_ref, got_ref, q_ref, acc_ref, m_ref, count_ref, list_ref, keys, values
):
    for s in range(8):
        at = pl.ds(s * 64, 64)
        keys[at, :] = got_ref[s, :, 768:896]
        values[at, 0:D] = got_ref[s, :, 896:1024]
    values[:, D:] = jnp.ones((512, D), jnp.bfloat16)
    q_ref[NR * ROWS :, :] = jnp.zeros((ROWS, D), jnp.bfloat16)
    m_ref[NR * ROWS :, :] = jnp.zeros((ROWS, D), jnp.float32)
    acc_ref[NR * ROWS :, :] = jnp.zeros((ROWS, 2 * D), jnp.float32)
    for p in range(PLACES + 1):
        count_ref[p] = 0
    row = lax.broadcasted_iota(jnp.int32, (RESP * ROWS, RESP * T), 0)
    col = lax.broadcasted_iota(jnp.int32, (RESP * ROWS, RESP * T), 1)
    seen = (row // ROWS == col // T) & (row % T >= col % T)

    @pl.loop(0, 4)
    def _(pair):
        for k in range(8 * TOPK):
            r = pair * 8 + k // TOPK
            place = at_ref[ids_ref[r, k % TOPK]]
            rank = count_ref[place]
            list_ref[place, rank] = r
            count_ref[place] = rank + 1
        two = [pair * 2, pair * 2 + 1]
        q = [
            jnp.concatenate(
                [
                    got_ref[s, a * T : (a + 1) * T, g * D : (g + 1) * D]
                    for a in range(RESP)
                    for g in range(GROUP)
                ],
                axis=0,
            )
            for s in two
        ]
        own = [
            jnp.where(seen, nt(q[i], got_ref[s, :, 512:640]), -jnp.inf) for i, s in enumerate(two)
        ]
        far = [nt(q[i], keys[...]) for i in range(2)]
        m = []
        for i in range(2):
            top = jnp.maximum(
                jnp.max(far[i], axis=1, keepdims=True), jnp.max(own[i], axis=1, keepdims=True)
            )
            m.append(jnp.broadcast_to(top * COEF, (RESP * ROWS, D)))
        for i, s in enumerate(two):
            at = pl.ds(pl.multiple_of(s * (RESP * ROWS), RESP * ROWS), RESP * ROWS)
            p = jnp.concatenate(
                [
                    jnp.exp2(far[i][:, j * D : (j + 1) * D] * COEF - m[i]).astype(jnp.bfloat16)
                    for j in range(4)
                ],
                axis=1,
            )
            po = jnp.exp2(own[i] * COEF - m[i][:, : RESP * T]).astype(jnp.bfloat16)
            vo = jnp.concatenate(
                [got_ref[s, :, 640:768], jnp.ones((RESP * T, D), jnp.bfloat16)], axis=1
            )
            acc = jnp.dot(p, values[...], preferred_element_type=jnp.float32)
            q_ref[at, :] = q[i]
            m_ref[at, :] = m[i]
            acc_ref[at, :] = acc + jnp.dot(po, vo, preferred_element_type=jnp.float32)


def first_call(ids, location, got):
    n = SLOTS * ROWS
    vmem = pl.BlockSpec(memory_space=pltpu.VMEM)
    smem = pl.BlockSpec(memory_space=pltpu.SMEM)
    return pl.pallas_call(
        first_kernel,
        out_shape=(
            jax.ShapeDtypeStruct((n, D), jnp.bfloat16),
            jax.ShapeDtypeStruct((n, 2 * D), jnp.float32),
            jax.ShapeDtypeStruct((n, D), jnp.float32),
            jax.ShapeDtypeStruct((PLACES + 1,), jnp.int32),
            jax.ShapeDtypeStruct((PLACES + 1, NR), jnp.int32),
        ),
        in_specs=[smem] * 2 + [vmem],
        out_specs=(vmem,) * 3 + (smem,) * 2,
        scratch_shapes=[
            pltpu.VMEM((512, D), jnp.bfloat16),
            pltpu.VMEM((512, 2 * D), jnp.bfloat16),
        ],
        compiler_params=pltpu.CompilerParams(vmem_limit_bytes=16 * 1024 * 1024),
        cost_estimate=pl.CostEstimate(
            flops=8 * 2048 * 576 * D, bytes_accessed=6 * 1024 * 1024, transcendentals=2048 * 576
        ),
        name="prefix_and_own",
    )(ids, location, got)


def passage_kernel(rounds, n_blocks, prefix, last, spot_ref, count_ref, list_ref, q_ref, *rest):
    blocks = rest[2 : 2 + n_blocks]
    acc, m = rest[2 + n_blocks : 4 + n_blocks]
    ones = jnp.ones((256, D), jnp.bfloat16)
    if prefix:
        run_prefix(blocks[-1], ones, q_ref, acc, m)
    for streams in rounds:
        run_streams(streams, blocks, ones, spot_ref, count_ref, list_ref, q_ref, acc, m)
    if last:
        out_ref = rest[4 + n_blocks]

        @pl.loop(0, NR, unroll=4)
        def _(r):
            at = pl.ds(pl.multiple_of(r * ROWS, ROWS), ROWS)
            o = (acc[at, 0:D] / acc[at, D:]).astype(jnp.bfloat16)
            for g in range(GROUP):
                out_ref[pl.ds(pl.multiple_of(r * T, T), T), g * D : (g + 1) * D] = o[
                    g * T : (g + 1) * T
                ]


def attend(rows, halves, ones, q_ref, acc, m):
    at = [[pl.ds(pl.multiple_of(r * ROWS, ROWS), ROWS) for r in rows[s]] for s in range(2)]
    sc, keep = [], []
    for s in range(2):
        q = jnp.concatenate([q_ref[a, :] for a in at[s]], axis=0)
        sc.append([nt(q, h[:, 0:D]) for h in halves[s]])
        keep.append([jnp.concatenate([h[:, D:], ones], axis=1) for h in halves[s]])
    new, shrink = [], []
    for s in range(2):
        top = jnp.maximum(
            jnp.max(sc[s][0], axis=1, keepdims=True), jnp.max(sc[s][1], axis=1, keepdims=True)
        )
        old = jnp.concatenate([m[a, :] for a in at[s]], axis=0)
        new.append(jnp.maximum(old, top * COEF))
        shrink.append(jnp.exp2(old - new[s]))
        for k, a in enumerate(at[s]):
            m[a, :] = new[s][k * ROWS : (k + 1) * ROWS]
    mixed = []
    for s in range(2):
        mixed.append(0)
        for h in range(2):
            p = jnp.concatenate(
                [
                    jnp.exp2(sc[s][h][:, j * D : (j + 1) * D] * COEF - new[s]).astype(jnp.bfloat16)
                    for j in range(2)
                ],
                axis=1,
            )
            mixed[s] = mixed[s] + jnp.dot(p, keep[s][h], preferred_element_type=jnp.float32)
    for s in range(2):
        for k, a in enumerate(at[s]):
            part = slice(k * ROWS, (k + 1) * ROWS)
            acc[a, 0:D] = acc[a, 0:D] * shrink[s][part] + mixed[s][part, 0:D]
            acc[a, D:] = acc[a, D:] * shrink[s][part] + mixed[s][part, D:]


def run_prefix(rows_ref, ones, q_ref, acc, m):
    @pl.loop(0, NR // (2 * BATCH))
    def _(b):
        rows = [[(2 * b + s) * BATCH + k for k in range(BATCH)] for s in range(2)]
        attend(rows, [[rows_ref.at[0], rows_ref.at[1]]] * 2, ones, q_ref, acc, m)


def run_streams(streams, blocks, ones, spot_ref, count_ref, list_ref, q_ref, acc, m):
    def place_of(s, i):
        turn = any_turn(streams[s].base + i)
        up = spot_ref[1] + streams[s].offset
        return ((spot_ref[0] + turn) & (NY - 1)) * NZ + (up & (NZ - 1))

    def batches(s):
        total = 0
        for i in range(streams[s].count):
            total = total + jnp.maximum((count_ref[place_of(s, i)] + BATCH - 1) // BATCH, 1)
        return total

    def step(_, carry):
        rows, halves, ahead = [], [], []
        for s, (i, b) in enumerate(carry):
            i_here = jnp.minimum(i, streams[s].count - 1)
            place = jnp.where(i < streams[s].count, place_of(s, i_here), PLACES)
            count = count_ref[place]
            rows.append(
                [
                    jnp.where(b * BATCH + k < count, list_ref[place, b * BATCH + k], NR)
                    for k in range(BATCH)
                ]
            )
            full = (b + 1) * BATCH >= count
            ahead.append((i + full.astype(jnp.int32), jnp.where(full, 0, b + 1)))
            pair = streams[s].pair
            halves.append([h.at[streams[s].base + i_here] for h in blocks[2 * pair : 2 * pair + 2]])
        attend(rows, halves, ones, q_ref, acc, m)
        return tuple(ahead)

    start = ((jnp.int32(0), jnp.int32(0)),) * 2
    lax.fori_loop(0, jnp.maximum(batches(0), batches(1)), step, start)


def passage_call(spot, counts_of, lists, q, acc, m, rounds, pairs, prefix=None, last=False):
    n = SLOTS * ROWS
    total = sum(stream.count for streams in rounds for stream in streams)
    blocks = [a for pair in pairs for a in pair] + ([] if prefix is None else [prefix])
    out_shape = [
        jax.ShapeDtypeStruct((n, 2 * D), jnp.float32),
        jax.ShapeDtypeStruct((n, D), jnp.float32),
    ]
    if last:
        out_shape.append(jax.ShapeDtypeStruct((NR * T, GROUP * D), jnp.bfloat16))
    vmem = pl.BlockSpec(memory_space=pltpu.VMEM)
    smem = pl.BlockSpec(memory_space=pltpu.SMEM)
    return pl.pallas_call(
        functools.partial(passage_kernel, rounds, len(blocks), prefix is not None, last),
        out_shape=tuple(out_shape),
        in_specs=[smem] * 3 + [vmem] * (3 + len(blocks)),
        out_specs=(vmem,) * len(out_shape),
        input_output_aliases={4: 0, 5: 1},
        compiler_params=pltpu.CompilerParams(vmem_limit_bytes=20 * 1024 * 1024),
        cost_estimate=pl.CostEstimate(
            flops=16 * total * 10 * ROWS * 512 * D,
            bytes_accessed=6 * 1024 * 1024,
            transcendentals=total * 10 * ROWS * 512,
        ),
        name="passages",
    )(spot, counts_of, lists, q, acc, m, *blocks)


def per_device(
    queries,
    own_keys,
    own_values,
    prefix_keys,
    prefix_values,
    passage_keys,
    passage_values,
    retrieval,
    location,
):
    grp, dev = lax.axis_index("grp"), lax.axis_index("dev")
    x, c, y, z = grp >> 1, grp & 1, dev >> 3, dev & 7
    low = y & 1
    spot = jnp.stack([y, z])

    def two_heads(cache):
        return lax.dynamic_slice(cache[0], (c * 256, x * 2 * D), (256, 2 * D))

    k2, v2 = two_heads(passage_keys), two_heads(passage_values)
    even = jnp.concatenate([k2[:, :D], v2[:, :D]], axis=1)
    odd = jnp.concatenate([k2[:, D:], v2[:, D:]], axis=1)
    kept = jnp.where(low == 0, even, odd)
    given = jnp.where(low == 0, odd, even)
    ids = jnp.pad(retrieval.astype(jnp.bfloat16), ((0, 0), (0, D - TOPK)))
    ids = jnp.broadcast_to(ids[:, None, :], (RESP, T, D)).reshape(64, D)
    parcel = parcel_call(after(low, given), queries, own_keys, own_values, prefix_keys, prefix_values, ids)
    pieces = [kept, send(given, y_by(1)), send(given, y_by(-1)), send(kept, y_by(2))]
    pieces[3] = after(pieces[3], parcel)
    column = jnp.stack(pieces)
    def swap(block):
        return block, send(block, other_core)

    got = lax.all_to_all(after(parcel, column), AXES, 0, 0, tiled=True, axis_index_groups=head_groups())
    up1, down1 = send(column, z_by(1)), send(column, z_by(-1))
    up2, down2 = send(up1, z_by(1)), send(down1, z_by(-1))
    one = [swap(up1), swap(down1)]
    got = after(got, one[0][1], one[1][1])
    here = swap(after(column, got))
    theirs = send(got[:, :, 768:1024].reshape(2, 256, 2 * D), other_core)
    chosen = got[:, :, 1024 : 1024 + TOPK].reshape(NR, T, TOPK)[:, 0].astype(jnp.int32)
    q, acc, m, counts_of, lists = first_call(chosen, location, got)

    state = (spot, counts_of, lists, q)
    seen = (m, one[0][1], one[1][1])
    up3, down3 = send(after(up2, *seen), z_by(1)), send(after(down2, *seen), z_by(-1))
    two = [swap(after(up2, m)), swap(after(down2, m))]
    acc, m = passage_call(*state, acc, m, (split(0, 0), both(1, 1)), [here] + one, theirs)
    up3, down3 = after(up3, m), after(down3, m)
    four = send(jnp.where(c == 0, up3, down3), lambda x, c, y, z: (x, c, y, z + 1 - 2 * c))
    three = [swap(up3), swap(down3)]
    acc, m = passage_call(*state, acc, m, (both(0, 2),), two)
    acc, m = passage_call(*state, acc, m, (both(0, 3),), three)
    four = after(four, m)
    _, _, out = passage_call(*state, acc, m, (split(0, 4),), [swap(four)], last=True)

    out = out.reshape(KV, 64, GROUP * D)
    home = lax.all_to_all(out, AXES, 0, 0, tiled=True, axis_index_groups=head_groups())
    return home.transpose(1, 0, 2).reshape(RESP, T, HEADS * D)


def solution(mesh):
    placed = (
        P(("grp", "dev"), None, None),
        P(("grp", "dev"), None, None),
        P(("grp", "dev"), None, None),
        P("grp", None),
        P("grp", None),
        P("dev", None, None),
        P("dev", None, None),
        P(("grp", "dev"), None),
        P(),
    )
    return jax.shard_map(
        per_device,
        mesh=mesh,
        in_specs=placed,
        out_specs=P(("grp", "dev"), None, None),
        check_vma=False,
    )
```

```python
import functools
import math
import typing

import jax
import jax.numpy as jnp
from jax import lax
from jax.experimental import pallas as pl
from jax.experimental.pallas import tpu as pltpu
from jax.sharding import PartitionSpec as P

HEADS = 32
KV = 8
D = 128
TOPK = 8
NX, NC, NY, NZ = 4, 2, 4, 8
AXES = ("grp", "dev")
RESP = 4
T = 16
GROUP = HEADS // KV
ROWS = GROUP * T
NR = 8 * RESP
SLOTS = NR + 1
BATCH = 8
PLACES = 32
COEF = math.log2(math.e) / math.sqrt(D)


def index_of(x, c, y, z):
    return ((x % NX) * NC + c) * (NY * NZ) + (y % NY) * NZ + z % NZ


def moves(to):
    places = [
        (x, c, y, z) for x in range(NX) for c in range(NC) for y in range(NY) for z in range(NZ)
    ]
    return [(index_of(*p), index_of(*to(*p))) for p in places]


def send(block, to):
    return lax.ppermute(block, AXES, moves(to))


def after(block, *earlier):
    return lax.optimization_barrier((block, *earlier))[0]


def y_by(step):
    return lambda x, c, y, z: (x, c, y + step, z)


def z_by(step):
    return lambda x, c, y, z: (x, c, y, z + step * (1 - 2 * c))


def other_core(x, c, y, z):
    return (x, 1 - c, y, z)


def head_groups():
    return [
        [index_of(x, c, 2 * high + low, z) for x in range(NX) for low in range(2)]
        for c in range(NC)
        for high in range(2)
        for z in range(NZ)
    ]


class Stream(typing.NamedTuple):
    pair: int
    base: int
    count: int
    offset: int


def any_turn(i):
    return jnp.where(i < 2, -i, i - 1)


def split(pair, offset):
    return (Stream(pair, 0, 2, offset), Stream(pair, 2, 2, offset))


def both(pair, offset):
    return (Stream(pair, 0, 4, -offset), Stream(pair + 1, 0, 4, offset))


def nt(a, b):
    return lax.dot_general(a, b, (((1,), (1,)), ((), ())), preferred_element_type=jnp.float32)


def parcel_kernel(
    low_ref, q_hbm, ok_hbm, ov_hbm, pk_hbm, pv_hbm, ids_ref, out_ref, q, ok, ov, pk, pv, sems
):
    rows = pl.ds(pl.multiple_of(low_ref[0] * 64, 64), 64)
    pairs = [(ok_hbm, ok), (ov_hbm, ov), (pk_hbm.at[rows, :], pk), (pv_hbm.at[rows, :], pv)]
    copies = [pltpu.make_async_copy(*pair, sems.at[k]) for k, pair in enumerate(pairs + [(q_hbm, q)])]
    for copy in copies:
        copy.start()
    for h in range(KV):
        out_ref[h, :, 1024:1152] = ids_ref[...]
    for k, source in enumerate((ok, ov, pk, pv)):
        copies[k].wait()
        for h in range(KV):
            out_ref[h, :, 512 + k * D : 512 + (k + 1) * D] = source[:, h * D : (h + 1) * D]
    copies[4].wait()
    for h in range(KV):
        out_ref[h, :, 0:512] = q[:, h * 512 : (h + 1) * 512]


def parcel_call(low, queries, own_keys, own_values, prefix_keys, prefix_values, ids):
    anywhere = pl.BlockSpec(memory_space=pl.ANY)
    vmem = pl.BlockSpec(memory_space=pltpu.VMEM)
    return pl.pallas_call(
        parcel_kernel,
        out_shape=jax.ShapeDtypeStruct((KV, 64, 1152), jnp.bfloat16),
        in_specs=[pl.BlockSpec(memory_space=pltpu.SMEM)] + [anywhere] * 5 + [vmem],
        out_specs=vmem,
        scratch_shapes=[pltpu.VMEM((64, HEADS * D), jnp.bfloat16)]
        + [pltpu.VMEM((64, KV * D), jnp.bfloat16)] * 4
        + [pltpu.SemaphoreType.DMA((5,))],
        compiler_params=pltpu.CompilerParams(vmem_limit_bytes=8 * 1024 * 1024),
        cost_estimate=pl.CostEstimate(flops=0, bytes_accessed=6 * 1024 * 1024, transcendentals=0),
        name="parcel",
    )(
        low.reshape(1),
        queries.reshape(64, HEADS * D),
        own_keys.reshape(64, KV * D),
        own_values.reshape(64, KV * D),
        prefix_keys,
        prefix_values,
        ids,
    )


def first_kernel(
    ids_ref, at_ref, got_ref, q_ref, acc_ref, m_ref, count_ref, list_ref, keys, values
):
    for s in range(8):
        at = pl.ds(s * 64, 64)
        keys[at, :] = got_ref[s, :, 768:896]
        values[at, 0:D] = got_ref[s, :, 896:1024]
    values[:, D:] = jnp.ones((512, D), jnp.bfloat16)
    q_ref[NR * ROWS :, :] = jnp.zeros((ROWS, D), jnp.bfloat16)
    m_ref[NR * ROWS :, :] = jnp.zeros((ROWS, D), jnp.float32)
    acc_ref[NR * ROWS :, :] = jnp.zeros((ROWS, 2 * D), jnp.float32)
    for p in range(PLACES + 1):
        count_ref[p] = 0
    row = lax.broadcasted_iota(jnp.int32, (RESP * ROWS, RESP * T), 0)
    col = lax.broadcasted_iota(jnp.int32, (RESP * ROWS, RESP * T), 1)
    seen = (row // ROWS == col // T) & (row % T >= col % T)

    @pl.loop(0, 4)
    def _(pair):
        for k in range(8 * TOPK):
            r = pair * 8 + k // TOPK
            place = at_ref[ids_ref[r, k % TOPK]]
            rank = count_ref[place]
            list_ref[place, rank] = r
            count_ref[place] = rank + 1
        two = [pair * 2, pair * 2 + 1]
        q = [
            jnp.concatenate(
                [
                    got_ref[s, a * T : (a + 1) * T, g * D : (g + 1) * D]
                    for a in range(RESP)
                    for g in range(GROUP)
                ],
                axis=0,
            )
            for s in two
        ]
        own = [
            jnp.where(seen, nt(q[i], got_ref[s, :, 512:640]), -jnp.inf) for i, s in enumerate(two)
        ]
        far = [nt(q[i], keys[...]) for i in range(2)]
        m = []
        for i in range(2):
            top = jnp.maximum(
                jnp.max(far[i], axis=1, keepdims=True), jnp.max(own[i], axis=1, keepdims=True)
            )
            m.append(jnp.broadcast_to(top * COEF, (RESP * ROWS, D)))
        for i, s in enumerate(two):
            at = pl.ds(pl.multiple_of(s * (RESP * ROWS), RESP * ROWS), RESP * ROWS)
            p = jnp.concatenate(
                [
                    jnp.exp2(far[i][:, j * D : (j + 1) * D] * COEF - m[i]).astype(jnp.bfloat16)
                    for j in range(4)
                ],
                axis=1,
            )
            po = jnp.exp2(own[i] * COEF - m[i][:, : RESP * T]).astype(jnp.bfloat16)
            vo = jnp.concatenate(
                [got_ref[s, :, 640:768], jnp.ones((RESP * T, D), jnp.bfloat16)], axis=1
            )
            acc = jnp.dot(p, values[...], preferred_element_type=jnp.float32)
            q_ref[at, :] = q[i]
            m_ref[at, :] = m[i]
            acc_ref[at, :] = acc + jnp.dot(po, vo, preferred_element_type=jnp.float32)


def first_call(ids, location, got):
    n = SLOTS * ROWS
    vmem = pl.BlockSpec(memory_space=pltpu.VMEM)
    smem = pl.BlockSpec(memory_space=pltpu.SMEM)
    return pl.pallas_call(
        first_kernel,
        out_shape=(
            jax.ShapeDtypeStruct((n, D), jnp.bfloat16),
            jax.ShapeDtypeStruct((n, 2 * D), jnp.float32),
            jax.ShapeDtypeStruct((n, D), jnp.float32),
            jax.ShapeDtypeStruct((PLACES + 1,), jnp.int32),
            jax.ShapeDtypeStruct((PLACES + 1, NR), jnp.int32),
        ),
        in_specs=[smem] * 2 + [vmem],
        out_specs=(vmem,) * 3 + (smem,) * 2,
        scratch_shapes=[
            pltpu.VMEM((512, D), jnp.bfloat16),
            pltpu.VMEM((512, 2 * D), jnp.bfloat16),
        ],
        compiler_params=pltpu.CompilerParams(vmem_limit_bytes=16 * 1024 * 1024),
        cost_estimate=pl.CostEstimate(
            flops=8 * 2048 * 576 * D, bytes_accessed=6 * 1024 * 1024, transcendentals=2048 * 576
        ),
        name="prefix_and_own",
    )(ids, location, got)


def passage_kernel(rounds, n_blocks, prefix, last, spot_ref, count_ref, list_ref, q_ref, *rest):
    blocks = rest[2 : 2 + n_blocks]
    acc, m = rest[2 + n_blocks : 4 + n_blocks]
    ones = jnp.ones((256, D), jnp.bfloat16)
    if prefix:
        run_prefix(blocks[-1], ones, q_ref, acc, m)
    for streams in rounds:
        run_streams(streams, blocks, ones, spot_ref, count_ref, list_ref, q_ref, acc, m)
    if last:
        out_ref = rest[4 + n_blocks]

        @pl.loop(0, NR, unroll=4)
        def _(r):
            at = pl.ds(pl.multiple_of(r * ROWS, ROWS), ROWS)
            o = (acc[at, 0:D] / acc[at, D:]).astype(jnp.bfloat16)
            for g in range(GROUP):
                out_ref[pl.ds(pl.multiple_of(r * T, T), T), g * D : (g + 1) * D] = o[
                    g * T : (g + 1) * T
                ]


def attend(rows, halves, ones, q_ref, acc, m):
    at = [[pl.ds(pl.multiple_of(r * ROWS, ROWS), ROWS) for r in rows[s]] for s in range(2)]
    sc, keep = [], []
    for s in range(2):
        q = jnp.concatenate([q_ref[a, :] for a in at[s]], axis=0)
        sc.append([nt(q, h[:, 0:D]) for h in halves[s]])
        keep.append([jnp.concatenate([h[:, D:], ones], axis=1) for h in halves[s]])
    new, shrink = [], []
    for s in range(2):
        top = jnp.maximum(
            jnp.max(sc[s][0], axis=1, keepdims=True), jnp.max(sc[s][1], axis=1, keepdims=True)
        )
        old = jnp.concatenate([m[a, :] for a in at[s]], axis=0)
        new.append(jnp.maximum(old, top * COEF))
        shrink.append(jnp.exp2(old - new[s]))
        for k, a in enumerate(at[s]):
            m[a, :] = new[s][k * ROWS : (k + 1) * ROWS]
    mixed = []
    for s in range(2):
        mixed.append(0)
        for h in range(2):
            p = jnp.concatenate(
                [
                    jnp.exp2(sc[s][h][:, j * D : (j + 1) * D] * COEF - new[s]).astype(jnp.bfloat16)
                    for j in range(2)
                ],
                axis=1,
            )
            mixed[s] = mixed[s] + jnp.dot(p, keep[s][h], preferred_element_type=jnp.float32)
    for s in range(2):
        for k, a in enumerate(at[s]):
            part = slice(k * ROWS, (k + 1) * ROWS)
            acc[a, 0:D] = acc[a, 0:D] * shrink[s][part] + mixed[s][part, 0:D]
            acc[a, D:] = acc[a, D:] * shrink[s][part] + mixed[s][part, D:]


def run_prefix(rows_ref, ones, q_ref, acc, m):
    @pl.loop(0, NR // (2 * BATCH))
    def _(b):
        rows = [[(2 * b + s) * BATCH + k for k in range(BATCH)] for s in range(2)]
        attend(rows, [[rows_ref.at[0], rows_ref.at[1]]] * 2, ones, q_ref, acc, m)


def run_streams(streams, blocks, ones, spot_ref, count_ref, list_ref, q_ref, acc, m):
    def place_of(s, i):
        turn = any_turn(streams[s].base + i)
        up = spot_ref[1] + streams[s].offset * spot_ref[2]
        return ((spot_ref[0] + turn) & (NY - 1)) * NZ + (up & (NZ - 1))

    def batches(s):
        total = 0
        for i in range(streams[s].count):
            total = total + jnp.maximum((count_ref[place_of(s, i)] + BATCH - 1) // BATCH, 1)
        return total

    def step(_, carry):
        rows, halves, ahead = [], [], []
        for s, (i, b) in enumerate(carry):
            i_here = jnp.minimum(i, streams[s].count - 1)
            place = jnp.where(i < streams[s].count, place_of(s, i_here), PLACES)
            count = count_ref[place]
            rows.append(
                [
                    jnp.where(b * BATCH + k < count, list_ref[place, b * BATCH + k], NR)
                    for k in range(BATCH)
                ]
            )
            full = (b + 1) * BATCH >= count
            ahead.append((i + full.astype(jnp.int32), jnp.where(full, 0, b + 1)))
            pair = streams[s].pair
            halves.append([h.at[streams[s].base + i_here] for h in blocks[2 * pair : 2 * pair + 2]])
        attend(rows, halves, ones, q_ref, acc, m)
        return tuple(ahead)

    start = ((jnp.int32(0), jnp.int32(0)),) * 2
    lax.fori_loop(0, jnp.maximum(batches(0), batches(1)), step, start)


def passage_call(spot, counts_of, lists, q, acc, m, rounds, pairs, prefix=None, last=False):
    n = SLOTS * ROWS
    total = sum(stream.count for streams in rounds for stream in streams)
    blocks = [a for pair in pairs for a in pair] + ([] if prefix is None else [prefix])
    out_shape = [
        jax.ShapeDtypeStruct((n, 2 * D), jnp.float32),
        jax.ShapeDtypeStruct((n, D), jnp.float32),
    ]
    if last:
        out_shape.append(jax.ShapeDtypeStruct((NR * T, GROUP * D), jnp.bfloat16))
    vmem = pl.BlockSpec(memory_space=pltpu.VMEM)
    smem = pl.BlockSpec(memory_space=pltpu.SMEM)
    return pl.pallas_call(
        functools.partial(passage_kernel, rounds, len(blocks), prefix is not None, last),
        out_shape=tuple(out_shape),
        in_specs=[smem] * 3 + [vmem] * (3 + len(blocks)),
        out_specs=(vmem,) * len(out_shape),
        input_output_aliases={4: 0, 5: 1},
        compiler_params=pltpu.CompilerParams(vmem_limit_bytes=20 * 1024 * 1024),
        cost_estimate=pl.CostEstimate(
            flops=16 * total * 10 * ROWS * 512 * D,
            bytes_accessed=6 * 1024 * 1024,
            transcendentals=total * 10 * ROWS * 512,
        ),
        name="passages",
    )(spot, counts_of, lists, q, acc, m, *blocks)


def per_device(
    queries,
    own_keys,
    own_values,
    prefix_keys,
    prefix_values,
    passage_keys,
    passage_values,
    retrieval,
    location,
):
    grp, dev = lax.axis_index("grp"), lax.axis_index("dev")
    x, c, y, z = grp >> 1, grp & 1, dev >> 3, dev & 7
    low = y & 1
    spot = jnp.stack([y, z, 1 - 2 * c])

    def two_heads(cache):
        return lax.dynamic_slice(cache[0], (c * 256, x * 2 * D), (256, 2 * D))

    k2, v2 = two_heads(passage_keys), two_heads(passage_values)
    even = jnp.concatenate([k2[:, :D], v2[:, :D]], axis=1)
    odd = jnp.concatenate([k2[:, D:], v2[:, D:]], axis=1)
    kept = jnp.where(low == 0, even, odd)
    given = jnp.where(low == 0, odd, even)
    ids = jnp.pad(retrieval.astype(jnp.bfloat16), ((0, 0), (0, D - TOPK)))
    ids = jnp.broadcast_to(ids[:, None, :], (RESP, T, D)).reshape(64, D)
    parcel = parcel_call(after(low, given), queries, own_keys, own_values, prefix_keys, prefix_values, ids)
    pieces = [kept, send(given, y_by(1)), send(given, y_by(-1)), send(kept, y_by(2))]
    pieces[3] = after(pieces[3], parcel)
    column = jnp.stack(pieces)
    def swap(block):
        return block, send(block, other_core)

    def cross(up, down):
        return [(up, send(down, other_core)), (down, send(up, other_core))]

    got = lax.all_to_all(after(parcel, column), AXES, 0, 0, tiled=True, axis_index_groups=head_groups())
    up1, down1 = send(column, z_by(1)), send(column, z_by(-1))
    up2, down2 = send(up1, z_by(1)), send(down1, z_by(-1))
    one = cross(up1, down1)
    got = after(got, one[0][1], one[1][1])
    here = swap(after(column, got))
    theirs = send(got[:, :, 768:1024].reshape(2, 256, 2 * D), other_core)
    chosen = got[:, :, 1024 : 1024 + TOPK].reshape(NR, T, TOPK)[:, 0].astype(jnp.int32)
    q, acc, m, counts_of, lists = first_call(chosen, location, got)

    state = (spot, counts_of, lists, q)
    seen = (m, one[0][1], one[1][1])
    up3, down3 = send(after(up2, *seen), z_by(1)), send(after(down2, *seen), z_by(-1))
    two = cross(after(up2, m), after(down2, m))
    acc, m = passage_call(*state, acc, m, (split(0, 0), both(1, 1)), [here] + one, theirs)
    up3, down3 = after(up3, m), after(down3, m)
    four = send(up3, z_by(1))
    three = cross(up3, down3)
    acc, m = passage_call(*state, acc, m, (both(0, 2),), two)
    acc, m = passage_call(*state, acc, m, (both(0, 3),), three)
    four = after(four, m)
    _, _, out = passage_call(*state, acc, m, (split(0, 4),), [swap(four)], last=True)

    out = out.reshape(KV, 64, GROUP * D)
    home = lax.all_to_all(out, AXES, 0, 0, tiled=True, axis_index_groups=head_groups())
    return home.transpose(1, 0, 2).reshape(RESP, T, HEADS * D)


def solution(mesh):
    placed = (
        P(("grp", "dev"), None, None),
        P(("grp", "dev"), None, None),
        P(("grp", "dev"), None, None),
        P("grp", None),
        P("grp", None),
        P("dev", None, None),
        P("dev", None, None),
        P(("grp", "dev"), None),
        P(),
    )
    return jax.shard_map(
        per_device,
        mesh=mesh,
        in_specs=placed,
        out_specs=P(("grp", "dev"), None, None),
        check_vma=False,
    )
```
